32 devices in a mesh: gx: 4 (over z), gy: 4 (over y, x), gz: 2 (over core).
Axes of the slice: x: 2, y: 2, z: 4, core: 2. Of those that a mesh axis runs over, the one named last changes fastest.
Arguments:
- features: bfloat16 [8192, 1024], P(('gx', 'gy', 'gz')), may hold values from -6 to 6
- cotangent: bfloat16 [8192, 1024], P(('gx', 'gy', 'gz')), may hold values from -6 to 6
- leaf_device: int32 [8192, 1], P(('gx', 'gy', 'gz')), may hold values from 0 to 31; in each aligned block of 256 rows (0 to 255, 256 to 511, ...) at most 16 rows name the same one
- neighbours: int32 [16, 16384], P(None, ('gx', 'gy', 'gz')), may hold values from 0 to 511
- radial: float32 [64, 16384], P(None, ('gx', 'gy', 'gz')), may hold values from 0.25 to 2
- first_zero: bfloat16 [256, 256], replicated, may hold values from -0.375 to 0.375
- first_one: bfloat16 [192, 192], replicated, may hold values from -0.4375 to 0.4375
- first_two: bfloat16 [128, 128], replicated, may hold values from -0.5 to 0.5
- first_three: bfloat16 [64, 64], replicated, may hold values from -0.75 to 0.75
- second_zero: bfloat16 [256, 256], replicated, may hold values from -0.375 to 0.375
- second_one: bfloat16 [192, 192], replicated, may hold values from -0.4375 to 0.4375
- second_two: bfloat16 [128, 128], replicated, may hold values from -0.5 to 0.5
- second_three: bfloat16 [64, 64], replicated, may hold values from -0.75 to 0.75
- lift_leaf: float32 [2, 16, 16], replicated, may hold values from -1 to 1
- lift_branch: float32 [4, 16, 16], replicated, may hold values from -0.75 to 0.75
- couple_root: float32 [4, 4, 16, 16], replicated, may hold values from -0.75 to 0.75
- couple_branch: float32 [4, 4, 16, 16], replicated, may hold values from -0.75 to 0.75
- couple_leaf: float32 [2, 2, 16, 16], replicated, may hold values from -1 to 1
Outputs:
- updated: bfloat16 [8192, 1024], P(('gx', 'gy', 'gz'))
- radial_grad: float32 [64, 16384], P(None, ('gx', 'gy', 'gz'))
The draws below stay inside these ranges and needn't reach their ends.
Inputs may be any that keep to these rules, and one draw needn't show every extreme that they name: `leaf_device`: among the 256 atoms of one brick at most 16 have the same leaf; every leaf holds at least one atom.
All inputs are finite; a program needn't handle non-finite values.
Results may differ from the reference program's by a relative error of at most 0.0037.
Values may be sent and summed in bfloat16 or wider, within the bound.
A program may use at most 64 MiB of HBM per device.

```python
import math
import jax
import jax.numpy as jnp
import numpy as np
from jax import lax

C = 64
F = 1024
NBR = 16
A_DEV = 256
ATOMS = 8192
CAP = 16
POOL = 512
POOLS = 16384
N_GX = 4
N_GY = 4
N_GZ = 2
DEVICES = 32


def touch_ends(values, own_key, smallest, largest):
    spot = [jax.random.randint(jax.random.fold_in(own_key, axis), (), 0, length) for axis, length in enumerate(values.shape)]
    main_axis = values.shape.index(max(values.shape))
    next_to = spot[:main_axis] + [(spot[main_axis] + 1) % values.shape[main_axis]] + spot[main_axis + 1:]
    return values.at[tuple(spot)].set(smallest).at[tuple(next_to)].set(largest)


def level_of(rng, dims, cuts, least, largest):
    gain, own = 1.0, jax.random.fold_in(rng, 6)
    for position, blocks in cuts:
        steps = jnp.exp(jax.random.uniform(jax.random.fold_in(own, position), (blocks,), jnp.float32, least / len(cuts), largest / len(cuts)))
        gain = gain * jnp.repeat(steps, dims[position] // blocks).reshape([-1 if axis == position else 1 for axis in range(len(dims))])
    return gain


def deal_out(key, own, number, rows, number_of, top, most, slope):
    sequence = jax.random.permutation(key, number_of)
    crowded, common = load_shares(number_of, rows * top, most, slope, True), load_shares(number_of, rows * top, most, slope, False)
    places = jnp.arange(number_of)

    def named(tallies, rotation):
        used = int((tallies > 0).sum())
        fixed = max(1, used // 4)
        passed = fixed + (places - fixed + rotation * (used - fixed)) % max(1, number_of - fixed)
        return jnp.zeros((number_of,), jnp.int32).at[sequence[jnp.where(places < fixed, places, passed)]].set(jnp.asarray(tallies, jnp.int32))

    tallies = jnp.where(number % 4 == 0, named(crowded, number // 4), named(common, number - number // 4 - 1))
    mixed = jax.random.permutation(jax.random.fold_in(own, 3), number_of)
    donor, taker = mixed[0:number_of // 2 * 2:2], mixed[1:number_of // 2 * 2:2]
    margin = jnp.minimum(tallies[donor] - 1, most - tallies[taker]) // 2
    margin = jnp.where((donor == sequence[0]) | (taker == sequence[0]) | (tallies[taker] == 0), 0, jnp.maximum(margin, 0))
    passed = jax.random.randint(jax.random.fold_in(own, 4), (number_of // 2,), 0, 1 << 20) % (margin + 1)
    tallies = tallies.at[donor].add(-passed).at[taker].add(passed)
    members = jnp.searchsorted(jnp.cumsum(tallies), jnp.arange(rows * top), side="right").astype(jnp.int32)
    table = members.reshape(top, rows).T
    table = table[jax.random.permutation(jax.random.fold_in(own, 1), rows)]
    rotation = jax.random.randint(jax.random.fold_in(own, 2), (rows, 1), 0, top)
    return jnp.take_along_axis(table, (jnp.arange(top)[None, :] + rotation) % top, axis=1)


def load_shares(count, total, bound, lean, full):
    loads = [(1 << 20) // math.isqrt(grade ** lean) + 1 for grade in range(1, count + 1)]
    largest = bound if full else min(bound, max(-(-total // count), total * loads[0] // sum(loads)))
    least = 1 if total - largest >= count - 1 else 0
    counts, rest = [largest] + [least] * (count - 1), total - largest - least * (count - 1)
    while rest > 0:
        movable = [i for i in range(1, count) if counts[i] < largest] or [i for i in range(1, count) if counts[i] < bound]
        pool, budget = sum([loads[i] for i in movable]), rest
        for i in movable:
            extra = min(bound - counts[i], max(1, budget * loads[i] // pool), rest)
            counts[i] = counts[i] + extra
            rest = rest - extra
    return np.array(counts)


def centred(rng, dims, scale, bound, cuts=(), held_as=jnp.bfloat16):
    loudness = level_of(rng, dims, cuts, -0.22, 0.18) if cuts else 1.0
    values = jax.random.normal(rng, dims, jnp.float32) * scale * loudness
    return jnp.minimum(jnp.maximum(values, -bound), bound).astype(held_as)


def setup_inputs(seed: int = 0) -> dict:
    arg_keys = jax.random.split(jax.random.key(seed), 19)
    features = centred(arg_keys[0], (ATOMS, F), 1.0, 6.0, ((0, 32),))
    cotangent = centred(arg_keys[1], (ATOMS, F), 1.0, 6.0, ((0, 32),))
    leaf_device_keys = jax.random.split(jax.random.fold_in(arg_keys[2], 1), ATOMS // A_DEV)
    leaf_device_turns = jax.random.permutation(jax.random.fold_in(arg_keys[2], 3), ATOMS // A_DEV)
    leaf_device = jax.vmap(lambda own, number: deal_out(jax.random.fold_in(arg_keys[2], 2), own, number, A_DEV, DEVICES, 1, CAP, 2))(leaf_device_keys, leaf_device_turns).reshape((ATOMS, 1))
    neighbours = touch_ends(jax.random.randint(arg_keys[3], (NBR, POOLS), 0, POOL), jax.random.fold_in(arg_keys[3], 1), 0, POOL - 1).astype(jnp.int32)
    radial = jnp.clip(jnp.exp(math.log(2.0) - 2.0794415 * jax.random.uniform(arg_keys[4], (NBR * 4, POOLS), jnp.float32) ** level_of(arg_keys[4], (NBR * 4, POOLS), ((1, 32),), -0.2, 0.2)), 0.25, 2.0)
    first_zero = centred(arg_keys[5], (4 * C, 4 * C), (4 * C) ** -0.5, 0.375)
    first_one = centred(arg_keys[6], (3 * C, 3 * C), (3 * C) ** -0.5, 0.4375)
    first_two = centred(arg_keys[7], (2 * C, 2 * C), (2 * C) ** -0.5, 0.5)
    first_three = centred(arg_keys[8], (C, C), C ** -0.5, 0.75)
    second_zero = centred(arg_keys[9], (4 * C, 4 * C), (4 * C) ** -0.5, 0.375)
    second_one = centred(arg_keys[10], (3 * C, 3 * C), (3 * C) ** -0.5, 0.4375)
    second_two = centred(arg_keys[11], (2 * C, 2 * C), (2 * C) ** -0.5, 0.5)
    second_three = centred(arg_keys[12], (C, C), C ** -0.5, 0.75)
    lift_leaf = centred(arg_keys[13], (N_GZ, 16, 16), (16 * N_GZ) ** -0.5, 1.0, (), jnp.float32)
    lift_branch = centred(arg_keys[14], (N_GY, 16, 16), (16 * N_GY) ** -0.5, 0.75, (), jnp.float32)
    couple_root = centred(arg_keys[15], (N_GX, N_GX, 16, 16), (16 * N_GX) ** -0.5, 0.75, (), jnp.float32)
    couple_branch = centred(arg_keys[16], (N_GY, N_GY, 16, 16), (16 * N_GY) ** -0.5, 0.75, (), jnp.float32)
    couple_leaf = centred(arg_keys[17], (N_GZ, N_GZ, 16, 16), (16 * N_GZ) ** -0.5, 1.0, (), jnp.float32)
    return dict(features=features, cotangent=cotangent, leaf_device=leaf_device, neighbours=neighbours, radial=radial, first_zero=first_zero, first_one=first_one, first_two=first_two, first_three=first_three, second_zero=second_zero, second_one=second_one, second_two=second_two, second_three=second_three, lift_leaf=lift_leaf, lift_branch=lift_branch, couple_root=couple_root, couple_branch=couple_branch, couple_leaf=couple_leaf)


DEGREES = (0, 1, 2, 3, 1, 2, 3, 1, 2, 3, 2, 3, 2, 3, 3, 3)

def mix_ref(values, mats, flip):
    chans = mats[3].shape[0]
    count = values.shape[0]
    form = 'rsk,jk->rsj' if flip else 'rsk,kj->rsj'
    pieces = [values[:, :4 * chans].reshape(count, 1, 4 * chans), values[:, 4 * chans:10 * chans].reshape(count, 2, 3 * chans), values[:, 10 * chans:14 * chans].reshape(count, 2, 2 * chans), values[:, 14 * chans:].reshape(count, 2, chans)]
    outs = []
    for piece, weight in zip(pieces, mats):
        result = jnp.einsum(form, piece.astype(jnp.float32), weight.astype(jnp.float32))
        outs.append(result.reshape(count, -1))
    return jnp.concatenate(outs, axis=1)

def leaf_work(pool_feat, pool_grad, nbrs, rads, local3, occ_int, firsts, seconds):
    count, width = pool_feat.shape
    chans = width // 16
    select = jnp.asarray(np.eye(4, dtype=np.float32)[list(DEGREES)])
    trans = mix_ref(pool_grad, seconds, True)
    order = jnp.argsort(1 - occ_int, stable=True).astype(jnp.int32)
    filled = jnp.sum(occ_int).astype(jnp.int32)
    occ = occ_int.astype(jnp.float32)

    def step(carry, item):
        choose, rad4 = item
        index = order[(choose % filled).astype(jnp.int32)]
        other = pool_feat[index]
        summed = pool_feat.astype(jnp.float32) + other.astype(jnp.float32)
        scales = rad4[np.array(DEGREES)].T
        zeta = (summed.reshape(count, 16, chans) * scales[:, :, None]).reshape(count, width).astype(jnp.bfloat16)
        upper = mix_ref(zeta, firsts, False)
        value = jax.nn.silu(upper).astype(jnp.bfloat16)
        message = mix_ref(value, seconds, False)
        sig = jax.nn.sigmoid(upper)
        grad_u = (sig * (1.0 + upper * (1.0 - sig)) * trans).astype(jnp.bfloat16)
        back = mix_ref(grad_u, firsts, True)
        per_coef = lax.optimization_barrier(jnp.sum((back * summed).reshape(count, 16, chans), axis=2))
        dradial = 0.25 * occ[:, None] * jnp.dot(per_coef, select, precision=lax.Precision.HIGHEST)
        return (carry + message, dradial.T)
    near, dr = lax.scan(step, jnp.zeros((count, width), jnp.float32), (nbrs, rads.reshape(-1, 4, count)))
    near = 0.25 * occ[:, None] * near
    feat = pool_feat.astype(jnp.float32)
    out = (feat + near + feat * local3.reshape(1, width)).astype(jnp.bfloat16)
    return (out, dr.reshape(-1, count))

def reference(features, cotangent, leaf_device, neighbours, radial, first_zero, first_one, first_two, first_three, second_zero, second_one, second_two, second_three, lift_leaf, lift_branch, couple_root, couple_branch, couple_leaf):
    hp = lax.Precision.HIGHEST
    target = leaf_device[:, 0].reshape(DEVICES, A_DEV)
    onehot = (target[:, :, None] == jnp.arange(DEVICES, dtype=jnp.int32)[None, None, :]).astype(jnp.int32)
    rank = lax.optimization_barrier(jnp.sum(jnp.cumsum(onehot, axis=1) * onehot, axis=2)) - 1
    source = jnp.arange(DEVICES, dtype=jnp.int32)[:, None]
    slot = (target * POOL + source * CAP + rank).reshape(ATOMS).astype(jnp.int32)
    occupied = jnp.zeros((DEVICES * POOL,), jnp.int32).at[slot].set(1).reshape(DEVICES, POOL)
    pool_feat = jnp.zeros((DEVICES * POOL, F), jnp.bfloat16).at[slot].set(features).reshape(DEVICES, POOL, F)
    pool_grad = jnp.zeros((DEVICES * POOL, F), jnp.bfloat16).at[slot].set(cotangent).reshape(DEVICES, POOL, F)
    leaf = (lax.optimization_barrier(jnp.sum(pool_feat, axis=1, dtype=jnp.float32)) / math.sqrt(A_DEV)).reshape(N_GX, N_GY, N_GZ, 16, C)
    mids = jnp.einsum('kpq,abkqc->abpc', lift_leaf, leaf, precision=hp)
    tops = jnp.einsum('bpq,abqc->apc', lift_branch, mids, precision=hp)
    root_mask = couple_root * (1.0 - jnp.eye(N_GX, dtype=jnp.float32))[:, :, None, None]
    branch_mask = couple_branch * (1.0 - jnp.eye(N_GY, dtype=jnp.float32))[:, :, None, None]
    leaf_mask = couple_leaf * (1.0 - jnp.eye(N_GZ, dtype=jnp.float32))[:, :, None, None]
    local1 = jnp.einsum('ajpq,jqc->apc', root_mask, tops, precision=hp)
    local2 = jnp.einsum('bqp,aqc->abpc', lift_branch, local1, precision=hp) + jnp.einsum('bjpq,ajqc->abpc', branch_mask, mids, precision=hp)
    local3 = jnp.einsum('kqp,abqc->abkpc', lift_leaf, local2, precision=hp) + jnp.einsum('kjpq,abjqc->abkpc', leaf_mask, leaf, precision=hp)
    local3 = local3.reshape(DEVICES, 16, C)
    nbr_dev = neighbours.reshape(NBR, DEVICES, POOL).transpose(1, 0, 2)
    rad_dev = radial.reshape(NBR * 4, DEVICES, POOL).transpose(1, 0, 2)
    firsts = (first_zero, first_one, first_two, first_three)
    seconds = (second_zero, second_one, second_two, second_three)

    def per_leaf(item):
        return leaf_work(item[0], item[1], item[2], item[3], item[4], item[5], firsts, seconds)
    pool_out, dr = lax.map(per_leaf, (pool_feat, pool_grad, nbr_dev, rad_dev, local3, occupied))
    updated = pool_out.reshape(DEVICES * POOL, F)[slot]
    radial_grad = dr.transpose(1, 0, 2).reshape(NBR * 4, POOLS)
    return (updated, radial_grad)
```

```python
import functools
import math

import jax
import jax.numpy as jnp
import numpy as np
from jax import lax
from jax.experimental import pallas as pl
from jax.experimental.pallas import tpu as pltpu
from jax.sharding import PartitionSpec as P

DEGREES = (0, 1, 2, 3, 1, 2, 3, 1, 2, 3, 2, 3, 2, 3, 3, 3)
AXES = ("gx", "gy", "gz")
GROUPS = ((0, 4), (4, 10), (10, 14), (14, 16))
TILE = 32
VMEM_LIMIT = 48 * 1024 * 1024


def degree_columns(chans):
    return np.repeat(np.asarray(DEGREES), chans)


def dotf(a, b, ca=1, cb=0):
    return lax.dot_general(a, b, (((ca,), (cb,)), ((), ())), preferred_element_type=jnp.float32)


def twice(matrix):
    zero = jnp.zeros_like(matrix)
    return jnp.concatenate(
        [jnp.concatenate([matrix, zero], 1), jnp.concatenate([zero, matrix], 1)], 0
    )


def edges(start, feat_ref, nbr_ref, rad_ref, spread_ref, nbr_count):
    pool = feat_ref.shape[0]
    lane = lax.broadcasted_iota(jnp.int32, (TILE, pool), 1)
    row = lax.broadcasted_iota(jnp.int32, (TILE, pool), 0) + start
    own = jnp.where(lane == row, 1.0, 0.0)
    nbr = nbr_ref[pl.ds(start, TILE), :].astype(jnp.int32)
    rad = rad_ref[pl.ds(start, TILE), :].astype(jnp.float32)
    half = 4 * nbr_count
    which = lax.broadcasted_iota(jnp.int32, (TILE, 2 * half), 1) % half // 4
    picks, rads = [], []
    for k in range(nbr_count):
        picks.append((own + jnp.where(lane == nbr[:, k : k + 1], 1.0, 0.0)).astype(jnp.bfloat16))
        rads.append(jnp.where(which == k, rad, 0.0).astype(jnp.bfloat16))
    y = dotf(jnp.concatenate(picks, 0), feat_ref[...])
    scale = dotf(jnp.concatenate(rads, 0), spread_ref[...])
    return y, (y * scale).astype(jnp.bfloat16)


def forward_kernel(
    nbr_count,
    chans,
    got_ref,
    nbrs_ref,
    radial_ref,
    spread_ref,
    f0, f1, f2, f3, s0, s1, s2, s3,
    base_ref,
    feat_ref,
    perm_ref,
    nbr_ref,
    rad_ref,
    count_ref,
):
    pool = got_ref.shape[0]
    width = 16 * chans
    ri = lax.broadcasted_iota(jnp.int32, (pool, pool), 0)
    ci = lax.broadcasted_iota(jnp.int32, (pool, pool), 1)
    mask = got_ref[:, width:]
    upto = dotf(mask, jnp.where(ri <= ci, 1.0, 0.0).astype(jnp.bfloat16), 0, 0)
    here = dotf(mask, jnp.where(ri == ci, 1.0, 0.0).astype(jnp.bfloat16), 0, 0)
    place = jnp.where(here[0:1] > 0.5, upto[0:1], 0.0) - 1.0
    perm = jnp.where(place.astype(jnp.int32) == ri, 1.0, 0.0).astype(jnp.bfloat16)
    perm_ref[...] = perm
    total = jnp.max(upto)
    count = total.astype(jnp.int32)
    count_ref[0, 0] = count
    feat_ref[...] = dotf(perm, got_ref[:, :width]).astype(jnp.bfloat16)
    raw = nbrs_ref[...].astype(jnp.float32)
    rest = raw - jnp.floor((raw + 0.5) / total) * total
    high = jnp.floor(rest * (1.0 / 32.0))
    low = rest - 32.0 * high
    nbr_ref[...] = 32.0 * dotf(perm, high.astype(jnp.bfloat16), 1, 1) + dotf(
        perm, low.astype(jnp.bfloat16), 1, 1
    )
    radial = radial_ref[...]
    coarse = radial.astype(jnp.bfloat16)
    fine = (radial - coarse.astype(jnp.float32)).astype(jnp.bfloat16)
    both = jnp.concatenate([coarse, fine], 0)
    rad_ref[...] = dotf(perm, both, 1, 1).astype(jnp.bfloat16)
    base_ref[...] = jnp.zeros_like(base_ref)

    def body(tile, carry):
        start = pl.multiple_of(tile * TILE, TILE)
        _, z = edges(start, feat_ref, nbr_ref, rad_ref, spread_ref, nbr_count)
        for (a, b), first, second in zip(GROUPS, (f0, f1, f2, f3), (s0, s1, s2, s3)):
            a, b = a * chans, b * chans
            u = dotf(z[:, a:b], first[...])
            v = u * (0.5 + 0.5 * jnp.tanh(0.5 * u))
            v = jnp.sum(v.reshape(nbr_count, TILE, b - a), axis=0)
            near = dotf(v.astype(jnp.bfloat16), second[...])
            own = feat_ref[pl.ds(start, TILE), a:b].astype(jnp.float32)
            base_ref[pl.ds(start, TILE), a:b] = own + 0.25 * near
        return carry

    lax.fori_loop(0, (count + TILE - 1) // TILE, body, 0)


def backward_kernel(
    nbr_count,
    chans,
    count_ref,
    got_ref,
    feat_ref,
    perm_ref,
    nbr_ref,
    rad_ref,
    spread_ref,
    gather_ref,
    f0, f1, f2, f3, s0, s1, s2, s3,
    out_ref,
    trans_ref,
    grad_ref,
):
    cot = dotf(perm_ref[...], got_ref[...]).astype(jnp.bfloat16)
    for (a, b), second in zip(GROUPS, (s0, s1, s2, s3)):
        a, b = a * chans, b * chans
        trans_ref[:, a:b] = dotf(cot[:, a:b], second[...], 1, 1)
    grad_ref[...] = jnp.zeros_like(grad_ref)
    count = count_ref[0, 0]
    cols = 4 * nbr_count

    def body(tile, carry):
        start = pl.multiple_of(tile * TILE, TILE)
        y, z = edges(start, feat_ref, nbr_ref, rad_ref, spread_ref, nbr_count)
        total = jnp.zeros((nbr_count * TILE, cols), jnp.float32)
        for (a, b), first in zip(GROUPS, (f0, f1, f2, f3)):
            a, b = a * chans, b * chans
            u = dotf(z[:, a:b], first[...])
            sig = 0.5 + 0.5 * jnp.tanh(0.5 * u)
            slope = sig * (1.0 + u * (1.0 - sig))
            t = trans_ref[pl.ds(start, TILE), a:b]
            gu = slope.reshape(nbr_count, TILE, b - a) * t[None]
            gu = gu.reshape(nbr_count * TILE, b - a).astype(jnp.bfloat16)
            prod = dotf(gu, first[...], 1, 1) * y[:, a:b]
            coarse = prod.astype(jnp.bfloat16)
            fine = (prod - coarse.astype(jnp.float32)).astype(jnp.bfloat16)
            total += dotf(coarse, gather_ref[a:b, :]) + dotf(fine, gather_ref[a:b, :])
        total = total.reshape(nbr_count, TILE, cols)
        k = lax.broadcasted_iota(jnp.int32, total.shape, 0)
        col = lax.broadcasted_iota(jnp.int32, total.shape, 2)
        total = jnp.sum(jnp.where(col // 4 == k, total, 0.0), axis=0)
        grad_ref[pl.ds(start, TILE), :] = 0.25 * total
        return carry

    lax.fori_loop(0, (count + TILE - 1) // TILE, body, 0)
    rest = grad_ref[...]
    perm = perm_ref[...]
    out = jnp.zeros(out_ref.shape, jnp.float32)
    for _ in range(3):
        piece = rest.astype(jnp.bfloat16)
        rest = rest - piece.astype(jnp.float32)
        out += dotf(piece, perm, 0, 0)
    out_ref[...] = out


def vmem(count):
    return [pl.BlockSpec(memory_space=pltpu.VMEM)] * count


def shards(
    features,
    cotangent,
    leaf_device,
    neighbours,
    radial,
    first_zero,
    first_one,
    first_two,
    first_three,
    second_zero,
    second_one,
    second_two,
    second_three,
    lift_leaf,
    lift_branch,
    couple_root,
    couple_branch,
    couple_leaf,
):
    hp = lax.Precision.HIGHEST
    bf16, f32 = jnp.bfloat16, jnp.float32
    rows, width = features.shape
    chans = width // 16
    size_x, size_y, size_z = (lax.axis_size(a) for a in AXES)
    devices = size_x * size_y * size_z
    nbr_count, pool = neighbours.shape
    cap = pool // devices

    target = leaf_device[:, 0]
    onehot = (target[:, None] == jnp.arange(devices, dtype=jnp.int32)[None, :]).astype(bf16)
    before = jnp.asarray(np.tril(np.ones((rows, rows), np.float32), -1), bf16)
    rank = jnp.sum(dotf(before, onehot) * onehot.astype(f32), axis=1).astype(jnp.int32)
    slot = target * cap + rank
    place = (slot[:, None] == jnp.arange(pool, dtype=jnp.int32)[None, :]).astype(bf16)

    def exchange(block):
        block = block.astype(bf16).reshape(devices, cap, block.shape[1])
        out = lax.all_to_all(block, AXES, split_axis=0, concat_axis=0, tiled=True)
        return out.reshape(pool, block.shape[2])

    marked = jnp.concatenate([features, jnp.ones((rows, 128), bf16)], axis=1)
    got_feat = exchange(dotf(place, marked, 0, 0))
    got_cot = exchange(dotf(place, cotangent, 0, 0))

    firsts = (first_zero, twice(first_one), twice(first_two), twice(first_three))
    seconds = (second_zero, twice(second_one), twice(second_two), twice(second_three))
    degrees = degree_columns(chans)
    cols = 4 * nbr_count
    match = (np.arange(cols)[:, None] % 4 == degrees[None, :]).astype(np.float32)
    spread = jnp.asarray(np.concatenate([match, match], 0), bf16)
    collect = jnp.asarray(match.T, bf16)

    shape = jax.ShapeDtypeStruct
    params = pltpu.CompilerParams(vmem_limit_bytes=VMEM_LIMIT)
    edge_flops = 2 * pool * nbr_count * width * 1024
    base, feat, perm, nbr, rad, count = pl.pallas_call(
        functools.partial(forward_kernel, nbr_count, chans),
        out_shape=(
            shape((pool, width), f32),
            shape((pool, width), bf16),
            shape((pool, pool), bf16),
            shape((pool, nbr_count), f32),
            shape((pool, 2 * cols), bf16),
            shape((1, 1), jnp.int32),
        ),
        in_specs=vmem(12),
        out_specs=tuple(vmem(5)) + (pl.BlockSpec(memory_space=pltpu.SMEM),),
        compiler_params=params,
        cost_estimate=pl.CostEstimate(
            flops=edge_flops, bytes_accessed=8 << 20, transcendentals=pool * nbr_count * width
        ),
        name="edge_forward",
    )(got_feat, neighbours, radial, spread, *firsts, *seconds)

    leaf = jnp.sum(got_feat[:, :width], axis=0, dtype=f32).reshape(16, chans) / math.sqrt(rows)
    tiles = lax.all_gather(leaf[None], AXES, axis=0, tiled=True)
    tiles = tiles.reshape(size_x, size_y, size_z, 16, chans)
    index_x, index_y, index_z = (lax.axis_index(a) for a in AXES)
    root_w = couple_root[index_x] * (jnp.arange(size_x) != index_x)[:, None, None]
    branch_w = couple_branch[index_y] * (jnp.arange(size_y) != index_y)[:, None, None]
    leaf_w = couple_leaf[index_z] * (jnp.arange(size_z) != index_z)[:, None, None]
    branches = jnp.einsum("zpq,xyzqc->xypc", lift_leaf, tiles, precision=hp)
    roots = jnp.einsum("ypq,xyqc->xpc", lift_branch, branches, precision=hp)
    local1 = jnp.einsum("xpq,xqc->pc", root_w, roots, precision=hp)
    local2 = jnp.einsum("qp,qc->pc", lift_branch[index_y], local1, precision=hp) + jnp.einsum(
        "ypq,yqc->pc", branch_w, branches[index_x], precision=hp
    )
    local3 = jnp.einsum("qp,qc->pc", lift_leaf[index_z], local2, precision=hp) + jnp.einsum(
        "zpq,zqc->pc", leaf_w, tiles[index_x, index_y], precision=hp
    )
    out_c = (base + feat.astype(f32) * local3.reshape(1, width)).astype(bf16)
    returned = exchange(dotf(perm, out_c, 0, 0))

    grads = pl.pallas_call(
        functools.partial(backward_kernel, nbr_count, chans),
        out_shape=shape((cols, pool), f32),
        in_specs=[pl.BlockSpec(memory_space=pltpu.SMEM)] + vmem(15),
        out_specs=vmem(1)[0],
        scratch_shapes=[pltpu.VMEM((pool, width), f32), pltpu.VMEM((pool, cols), f32)],
        compiler_params=params,
        cost_estimate=pl.CostEstimate(
            flops=2 * edge_flops, bytes_accessed=8 << 20, transcendentals=pool * nbr_count * width
        ),
        name="edge_backward",
    )(count, got_cot, feat, perm, nbr, rad, spread, collect, *firsts, *seconds)

    updated = dotf(place, returned).astype(bf16)
    return (updated, grads)


def solution(mesh):
    split = P(AXES, None)
    across = P(None, AXES)
    placed = (split, split, split, across, across) + (P(),) * 13
    return jax.shard_map(
        shards,
        mesh=mesh,
        in_specs=placed,
        out_specs=(split, across),
        check_vma=False,
    )
```

```python
import functools
import math

import jax
import jax.numpy as jnp
import numpy as np
from jax import lax
from jax.experimental import pallas as pl
from jax.experimental.pallas import tpu as pltpu
from jax.sharding import PartitionSpec as P

DEGREES = (0, 1, 2, 3, 1, 2, 3, 1, 2, 3, 2, 3, 2, 3, 3, 3)
AXES = ("gx", "gy", "gz")
GROUPS = ((0, 4), (4, 10), (10, 14), (14, 16))
TILE = 32
VMEM_LIMIT = 48 * 1024 * 1024


def degree_columns(chans):
    return np.repeat(np.asarray(DEGREES), chans)


def dotf(a, b, ca=1, cb=0):
    return lax.dot_general(a, b, (((ca,), (cb,)), ((), ())), preferred_element_type=jnp.float32)


def twice(matrix):
    zero = jnp.zeros_like(matrix)
    return jnp.concatenate(
        [jnp.concatenate([matrix, zero], 1), jnp.concatenate([zero, matrix], 1)], 0
    )


def packed(mats):
    blocks = [mats[0]] + [twice(m) for m in mats[1:]]
    widest = max(b.shape[1] for b in blocks)
    return jnp.concatenate([jnp.pad(b, ((0, 0), (0, widest - b.shape[1]))) for b in blocks], 0)


def edges(start, feat_ref, nbr_ref, rad_ref, spread_ref, nbr_count):
    pool = feat_ref.shape[0]
    lane = lax.broadcasted_iota(jnp.int32, (TILE, pool), 1)
    row = lax.broadcasted_iota(jnp.int32, (TILE, pool), 0) + start
    own = jnp.where(lane == row, 1.0, 0.0)
    nbr = nbr_ref[pl.ds(start, TILE), :].astype(jnp.int32)
    rad = rad_ref[pl.ds(start, TILE), :].astype(jnp.float32)
    half = 4 * nbr_count
    which = lax.broadcasted_iota(jnp.int32, (TILE, 2 * half), 1) % half // 4
    picks, rads = [], []
    for k in range(nbr_count):
        picks.append((own + jnp.where(lane == nbr[:, k : k + 1], 1.0, 0.0)).astype(jnp.bfloat16))
        rads.append(jnp.where(which == k, rad, 0.0).astype(jnp.bfloat16))
    y = dotf(jnp.concatenate(picks, 0), feat_ref[...])
    scale = dotf(jnp.concatenate(rads, 0), spread_ref[...])
    return y, (y * scale).astype(jnp.bfloat16)


def forward_kernel(
    nbr_count,
    chans,
    got_ref,
    nbrs_ref,
    radial_ref,
    spread_ref,
    first_ref,
    second_ref,
    base_ref,
    feat_ref,
    perm_ref,
    nbr_ref,
    rad_ref,
    count_ref,
):
    pool = got_ref.shape[0]
    width = 16 * chans
    ri = lax.broadcasted_iota(jnp.int32, (pool, pool), 0)
    ci = lax.broadcasted_iota(jnp.int32, (pool, pool), 1)
    mask = got_ref[:, width:]
    upto = dotf(mask, jnp.where(ri <= ci, 1.0, 0.0).astype(jnp.bfloat16), 0, 0)
    here = dotf(mask, jnp.where(ri == ci, 1.0, 0.0).astype(jnp.bfloat16), 0, 0)
    place = jnp.where(here[0:1] > 0.5, upto[0:1], 0.0) - 1.0
    perm = jnp.where(place.astype(jnp.int32) == ri, 1.0, 0.0).astype(jnp.bfloat16)
    perm_ref[...] = perm
    total = jnp.max(upto)
    count = total.astype(jnp.int32)
    count_ref[0, 0] = count
    feat_ref[...] = dotf(perm, got_ref[:, :width]).astype(jnp.bfloat16)
    raw = nbrs_ref[...].astype(jnp.float32)
    rest = raw - jnp.floor((raw + 0.5) / total) * total
    high = jnp.floor(rest * (1.0 / 32.0))
    low = rest - 32.0 * high
    nbr_ref[...] = 32.0 * dotf(perm, high.astype(jnp.bfloat16), 1, 1) + dotf(
        perm, low.astype(jnp.bfloat16), 1, 1
    )
    radial = radial_ref[...]
    coarse = radial.astype(jnp.bfloat16)
    fine = (radial - coarse.astype(jnp.float32)).astype(jnp.bfloat16)
    both = jnp.concatenate([coarse, fine], 0)
    rad_ref[...] = dotf(perm, both, 1, 1).astype(jnp.bfloat16)
    base_ref[...] = jnp.zeros_like(base_ref)

    def body(tile, carry):
        start = pl.multiple_of(tile * TILE, TILE)
        _, z = edges(start, feat_ref, nbr_ref, rad_ref, spread_ref, nbr_count)
        for a, b in GROUPS:
            a, b = a * chans, b * chans
            u = dotf(z[:, a:b], first_ref[a:b, : b - a])
            v = u * (0.5 + 0.5 * jnp.tanh(0.5 * u))
            v = jnp.sum(v.reshape(nbr_count, TILE, b - a), axis=0)
            near = dotf(v.astype(jnp.bfloat16), second_ref[a:b, : b - a])
            own = feat_ref[pl.ds(start, TILE), a:b].astype(jnp.float32)
            base_ref[pl.ds(start, TILE), a:b] = own + 0.25 * near
        return carry

    lax.fori_loop(0, (count + TILE - 1) // TILE, body, 0)


def backward_kernel(
    nbr_count,
    chans,
    count_ref,
    got_ref,
    feat_ref,
    perm_ref,
    nbr_ref,
    rad_ref,
    spread_ref,
    gather_ref,
    first_ref,
    second_ref,
    out_ref,
    trans_ref,
    grad_ref,
):
    cot = dotf(perm_ref[...], got_ref[:, : 16 * chans]).astype(jnp.bfloat16)
    for a, b in GROUPS:
        a, b = a * chans, b * chans
        trans_ref[:, a:b] = dotf(cot[:, a:b], second_ref[a:b, : b - a], 1, 1)
    grad_ref[...] = jnp.zeros_like(grad_ref)
    count = count_ref[0, 0]
    cols = 4 * nbr_count

    def body(tile, carry):
        start = pl.multiple_of(tile * TILE, TILE)
        y, z = edges(start, feat_ref, nbr_ref, rad_ref, spread_ref, nbr_count)
        total = jnp.zeros((nbr_count * TILE, cols), jnp.float32)
        for a, b in GROUPS:
            a, b = a * chans, b * chans
            u = dotf(z[:, a:b], first_ref[a:b, : b - a])
            sig = 0.5 + 0.5 * jnp.tanh(0.5 * u)
            slope = sig * (1.0 + u * (1.0 - sig))
            t = trans_ref[pl.ds(start, TILE), a:b]
            gu = slope.reshape(nbr_count, TILE, b - a) * t[None]
            gu = gu.reshape(nbr_count * TILE, b - a).astype(jnp.bfloat16)
            prod = dotf(gu, first_ref[a:b, : b - a], 1, 1) * y[:, a:b]
            coarse = prod.astype(jnp.bfloat16)
            fine = (prod - coarse.astype(jnp.float32)).astype(jnp.bfloat16)
            total += dotf(coarse, gather_ref[a:b, :]) + dotf(fine, gather_ref[a:b, :])
        total = total.reshape(nbr_count, TILE, cols)
        k = lax.broadcasted_iota(jnp.int32, total.shape, 0)
        col = lax.broadcasted_iota(jnp.int32, total.shape, 2)
        total = jnp.sum(jnp.where(col // 4 == k, total, 0.0), axis=0)
        grad_ref[pl.ds(start, TILE), :] = 0.25 * total
        return carry

    lax.fori_loop(0, (count + TILE - 1) // TILE, body, 0)
    rest = grad_ref[...]
    perm = perm_ref[...]
    out = jnp.zeros(out_ref.shape, jnp.float32)
    for _ in range(3):
        piece = rest.astype(jnp.bfloat16)
        rest = rest - piece.astype(jnp.float32)
        out += dotf(piece, perm, 0, 0)
    out_ref[...] = out


def vmem(count):
    return [pl.BlockSpec(memory_space=pltpu.VMEM)] * count


def shards(
    features,
    cotangent,
    leaf_device,
    neighbours,
    radial,
    first_zero,
    first_one,
    first_two,
    first_three,
    second_zero,
    second_one,
    second_two,
    second_three,
    lift_leaf,
    lift_branch,
    couple_root,
    couple_branch,
    couple_leaf,
):
    hp = lax.Precision.HIGHEST
    bf16, f32 = jnp.bfloat16, jnp.float32
    rows, width = features.shape
    chans = width // 16
    size_x, size_y, size_z = (lax.axis_size(a) for a in AXES)
    devices = size_x * size_y * size_z
    nbr_count, pool = neighbours.shape
    cap = pool // devices

    target = leaf_device[:, 0]
    onehot = (target[:, None] == jnp.arange(devices, dtype=jnp.int32)[None, :]).astype(bf16)
    before = jnp.asarray(np.tril(np.ones((rows, rows), np.float32), -1), bf16)
    rank = jnp.sum(dotf(before, onehot) * onehot.astype(f32), axis=1).astype(jnp.int32)
    slot = target * cap + rank
    place = (slot[:, None] == jnp.arange(pool, dtype=jnp.int32)[None, :]).astype(bf16)

    def exchange(block):
        block = block.astype(bf16).reshape(devices, cap, block.shape[1])
        out = lax.all_to_all(block, AXES, split_axis=0, concat_axis=0, tiled=True)
        return out.reshape(pool, block.shape[2])

    marked = jnp.concatenate([features, jnp.ones((rows, 128), bf16)], axis=1)
    got_feat = exchange(dotf(place, marked, 0, 0))
    leaf = jnp.sum(got_feat[:, :width], axis=0, dtype=f32) / math.sqrt(rows)
    coarse = lax.reduce_precision(leaf, 8, 7)
    halves = jnp.concatenate([coarse, leaf - coarse]).astype(bf16).reshape(1, cap, -1)
    halves = jnp.broadcast_to(halves, (devices,) + halves.shape[1:]).reshape(pool, -1)
    got_cot = exchange(
        jnp.concatenate([dotf(place, cotangent, 0, 0).astype(bf16), halves], axis=1)
    )

    firsts = packed((first_zero, first_one, first_two, first_three))
    seconds = packed((second_zero, second_one, second_two, second_three))
    degrees = degree_columns(chans)
    cols = 4 * nbr_count
    match = (np.arange(cols)[:, None] % 4 == degrees[None, :]).astype(np.float32)
    spread = jnp.asarray(np.concatenate([match, match], 0), bf16)
    collect = jnp.asarray(match.T, bf16)

    shape = jax.ShapeDtypeStruct
    params = pltpu.CompilerParams(vmem_limit_bytes=VMEM_LIMIT)
    edge_flops = 2 * pool * nbr_count * width * 1024
    base, feat, perm, nbr, rad, count = pl.pallas_call(
        functools.partial(forward_kernel, nbr_count, chans),
        out_shape=(
            shape((pool, width), f32),
            shape((pool, width), bf16),
            shape((pool, pool), bf16),
            shape((pool, nbr_count), f32),
            shape((pool, 2 * cols), bf16),
            shape((1, 1), jnp.int32),
        ),
        in_specs=vmem(6),
        out_specs=tuple(vmem(5)) + (pl.BlockSpec(memory_space=pltpu.SMEM),),
        compiler_params=params,
        cost_estimate=pl.CostEstimate(
            flops=edge_flops, bytes_accessed=8 << 20, transcendentals=pool * nbr_count * width
        ),
        name="edge_forward",
    )(got_feat, neighbours, radial, spread, firsts, seconds)

    tiles = jnp.sum(got_cot[:, width:].reshape(devices, 2, width), axis=1, dtype=f32)
    tiles = tiles.reshape(size_x, size_y, size_z, 16, chans)
    index_x, index_y, index_z = (lax.axis_index(a) for a in AXES)
    root_w = couple_root[index_x] * (jnp.arange(size_x) != index_x)[:, None, None]
    branch_w = couple_branch[index_y] * (jnp.arange(size_y) != index_y)[:, None, None]
    leaf_w = couple_leaf[index_z] * (jnp.arange(size_z) != index_z)[:, None, None]
    branches = jnp.einsum("zpq,xyzqc->xypc", lift_leaf, tiles, precision=hp)
    roots = jnp.einsum("ypq,xyqc->xpc", lift_branch, branches, precision=hp)
    local1 = jnp.einsum("xpq,xqc->pc", root_w, roots, precision=hp)
    local2 = jnp.einsum("qp,qc->pc", lift_branch[index_y], local1, precision=hp) + jnp.einsum(
        "ypq,yqc->pc", branch_w, branches[index_x], precision=hp
    )
    local3 = jnp.einsum("qp,qc->pc", lift_leaf[index_z], local2, precision=hp) + jnp.einsum(
        "zpq,zqc->pc", leaf_w, tiles[index_x, index_y], precision=hp
    )
    out_c = (base + feat.astype(f32) * local3.reshape(1, width)).astype(bf16)
    returned = exchange(dotf(perm, out_c, 0, 0))

    grads = pl.pallas_call(
        functools.partial(backward_kernel, nbr_count, chans),
        out_shape=shape((cols, pool), f32),
        in_specs=[pl.BlockSpec(memory_space=pltpu.SMEM)] + vmem(9),
        out_specs=vmem(1)[0],
        scratch_shapes=[pltpu.VMEM((pool, width), f32), pltpu.VMEM((pool, cols), f32)],
        compiler_params=params,
        cost_estimate=pl.CostEstimate(
            flops=2 * edge_flops, bytes_accessed=8 << 20, transcendentals=pool * nbr_count * width
        ),
        name="edge_backward",
    )(count, got_cot, feat, perm, nbr, rad, spread, collect, firsts, seconds)

    updated = dotf(place, returned).astype(bf16)
    return (updated, grads)


def solution(mesh):
    split = P(AXES, None)
    across = P(None, AXES)
    placed = (split, split, split, across, across) + (P(),) * 13
    return jax.shard_map(
        shards,
        mesh=mesh,
        in_specs=placed,
        out_specs=(split, across),
        check_vma=False,
    )
```

```python
import functools
import math

import jax
import jax.numpy as jnp
import numpy as np
from jax import lax
from jax.experimental import pallas as pl
from jax.experimental.pallas import tpu as pltpu
from jax.sharding import PartitionSpec as P

DEGREES = (0, 1, 2, 3, 1, 2, 3, 1, 2, 3, 2, 3, 2, 3, 3, 3)
AXES = ("gx", "gy", "gz")
GROUPS = ((0, 4), (4, 10), (10, 14), (14, 16))
TILE = 64
VMEM_LIMIT = 48 * 1024 * 1024


def degree_columns(chans):
    return np.repeat(np.asarray(DEGREES), chans)


def dotf(a, b, ca=1, cb=0):
    return lax.dot_general(a, b, (((ca,), (cb,)), ((), ())), preferred_element_type=jnp.float32)


def twice(matrix):
    zero = jnp.zeros_like(matrix)
    return jnp.concatenate(
        [jnp.concatenate([matrix, zero], 1), jnp.concatenate([zero, matrix], 1)], 0
    )


def packed(mats):
    blocks = [mats[0]] + [twice(m) for m in mats[1:]]
    widest = max(b.shape[1] for b in blocks)
    return jnp.concatenate([jnp.pad(b, ((0, 0), (0, widest - b.shape[1]))) for b in blocks], 0)


def edges(start, feat_ref, nbr_ref, rad_ref, spread_ref, nbr_count):
    pool = feat_ref.shape[0]
    lane = lax.broadcasted_iota(jnp.int32, (TILE, pool), 1)
    row = lax.broadcasted_iota(jnp.int32, (TILE, pool), 0) + start
    own = jnp.where(lane == row, 1.0, 0.0)
    nbr = nbr_ref[pl.ds(start, TILE), :].astype(jnp.int32)
    rad = rad_ref[pl.ds(start, TILE), :].astype(jnp.float32)
    half = 4 * nbr_count
    which = lax.broadcasted_iota(jnp.int32, (TILE, 2 * half), 1) % half // 4
    picks, rads = [], []
    for k in range(nbr_count):
        picks.append((own + jnp.where(lane == nbr[:, k : k + 1], 1.0, 0.0)).astype(jnp.bfloat16))
        rads.append(jnp.where(which == k, rad, 0.0).astype(jnp.bfloat16))
    y = dotf(jnp.concatenate(picks, 0), feat_ref[...])
    scale = dotf(jnp.concatenate(rads, 0), spread_ref[...])
    return y, (y * scale).astype(jnp.bfloat16)


def forward_kernel(
    nbr_count,
    chans,
    got_ref,
    nbrs_ref,
    radial_ref,
    spread_ref,
    first_ref,
    second_ref,
    base_ref,
    feat_ref,
    perm_ref,
    nbr_ref,
    rad_ref,
    count_ref,
):
    pool = got_ref.shape[0]
    width = 16 * chans
    ri = lax.broadcasted_iota(jnp.int32, (pool, pool), 0)
    ci = lax.broadcasted_iota(jnp.int32, (pool, pool), 1)
    mask = got_ref[:, width:]
    upto = dotf(mask, jnp.where(ri <= ci, 1.0, 0.0).astype(jnp.bfloat16), 0, 0)
    here = dotf(mask, jnp.where(ri == ci, 1.0, 0.0).astype(jnp.bfloat16), 0, 0)
    place = jnp.where(here[0:1] > 0.5, upto[0:1], 0.0) - 1.0
    perm = jnp.where(place.astype(jnp.int32) == ri, 1.0, 0.0).astype(jnp.bfloat16)
    perm_ref[...] = perm
    total = jnp.max(upto)
    count = total.astype(jnp.int32)
    count_ref[0, 0] = count
    feat_ref[...] = dotf(perm, got_ref[:, :width]).astype(jnp.bfloat16)
    raw = nbrs_ref[...].astype(jnp.float32)
    rest = raw - jnp.floor((raw + 0.5) / total) * total
    high = jnp.floor(rest * (1.0 / 32.0))
    low = rest - 32.0 * high
    nbr_ref[...] = 32.0 * dotf(perm, high.astype(jnp.bfloat16), 1, 1) + dotf(
        perm, low.astype(jnp.bfloat16), 1, 1
    )
    radial = radial_ref[...]
    coarse = radial.astype(jnp.bfloat16)
    fine = (radial - coarse.astype(jnp.float32)).astype(jnp.bfloat16)
    both = jnp.concatenate([coarse, fine], 0)
    rad_ref[...] = dotf(perm, both, 1, 1).astype(jnp.bfloat16)
    base_ref[...] = jnp.zeros_like(base_ref)

    def body(tile, carry):
        start = pl.multiple_of(tile * TILE, TILE)
        _, z = edges(start, feat_ref, nbr_ref, rad_ref, spread_ref, nbr_count)
        for a, b in GROUPS:
            a, b = a * chans, b * chans
            u = dotf(z[:, a:b], first_ref[a:b, : b - a])
            v = u * (0.5 + 0.5 * jnp.tanh(0.5 * u))
            v = jnp.sum(v.reshape(nbr_count, TILE, b - a), axis=0)
            near = dotf(v.astype(jnp.bfloat16), second_ref[a:b, : b - a])
            own = feat_ref[pl.ds(start, TILE), a:b].astype(jnp.float32)
            base_ref[pl.ds(start, TILE), a:b] = own + 0.25 * near
        return carry

    lax.fori_loop(0, (count + TILE - 1) // TILE, body, 0)


def backward_kernel(
    nbr_count,
    chans,
    count_ref,
    got_ref,
    feat_ref,
    perm_ref,
    nbr_ref,
    rad_ref,
    spread_ref,
    gather_ref,
    first_ref,
    second_ref,
    out_ref,
    trans_ref,
    grad_ref,
):
    cot = dotf(perm_ref[...], got_ref[:, : 16 * chans]).astype(jnp.bfloat16)
    for a, b in GROUPS:
        a, b = a * chans, b * chans
        trans_ref[:, a:b] = dotf(cot[:, a:b], second_ref[a:b, : b - a], 1, 1)
    grad_ref[...] = jnp.zeros_like(grad_ref)
    count = count_ref[0, 0]
    cols = 4 * nbr_count

    def body(tile, carry):
        start = pl.multiple_of(tile * TILE, TILE)
        y, z = edges(start, feat_ref, nbr_ref, rad_ref, spread_ref, nbr_count)
        total = jnp.zeros((nbr_count * TILE, cols), jnp.float32)
        for a, b in GROUPS:
            a, b = a * chans, b * chans
            u = dotf(z[:, a:b], first_ref[a:b, : b - a])
            sig = 0.5 + 0.5 * jnp.tanh(0.5 * u)
            slope = sig * (1.0 + u * (1.0 - sig))
            t = trans_ref[pl.ds(start, TILE), a:b]
            gu = slope.reshape(nbr_count, TILE, b - a) * t[None]
            gu = gu.reshape(nbr_count * TILE, b - a).astype(jnp.bfloat16)
            prod = dotf(gu, first_ref[a:b, : b - a], 1, 1) * y[:, a:b]
            coarse = prod.astype(jnp.bfloat16)
            fine = (prod - coarse.astype(jnp.float32)).astype(jnp.bfloat16)
            total += dotf(coarse, gather_ref[a:b, :]) + dotf(fine, gather_ref[a:b, :])
        total = total.reshape(nbr_count, TILE, cols)
        k = lax.broadcasted_iota(jnp.int32, total.shape, 0)
        col = lax.broadcasted_iota(jnp.int32, total.shape, 2)
        total = jnp.sum(jnp.where(col // 4 == k, total, 0.0), axis=0)
        grad_ref[pl.ds(start, TILE), :] = 0.25 * total
        return carry

    lax.fori_loop(0, (count + TILE - 1) // TILE, body, 0)
    rest = grad_ref[...]
    perm = perm_ref[...]
    out = jnp.zeros(out_ref.shape, jnp.float32)
    for _ in range(3):
        piece = rest.astype(jnp.bfloat16)
        rest = rest - piece.astype(jnp.float32)
        out += dotf(piece, perm, 0, 0)
    out_ref[...] = out


def vmem(count):
    return [pl.BlockSpec(memory_space=pltpu.VMEM)] * count


def shards(
    features,
    cotangent,
    leaf_device,
    neighbours,
    radial,
    first_zero,
    first_one,
    first_two,
    first_three,
    second_zero,
    second_one,
    second_two,
    second_three,
    lift_leaf,
    lift_branch,
    couple_root,
    couple_branch,
    couple_leaf,
):
    hp = lax.Precision.HIGHEST
    bf16, f32 = jnp.bfloat16, jnp.float32
    rows, width = features.shape
    chans = width // 16
    size_x, size_y, size_z = (lax.axis_size(a) for a in AXES)
    devices = size_x * size_y * size_z
    nbr_count, pool = neighbours.shape
    cap = pool // devices

    target = leaf_device[:, 0]
    onehot = (target[:, None] == jnp.arange(devices, dtype=jnp.int32)[None, :]).astype(bf16)
    before = jnp.asarray(np.tril(np.ones((rows, rows), np.float32), -1), bf16)
    rank = jnp.sum(dotf(before, onehot) * onehot.astype(f32), axis=1).astype(jnp.int32)
    slot = target * cap + rank
    place = (slot[:, None] == jnp.arange(pool, dtype=jnp.int32)[None, :]).astype(bf16)

    def exchange(block):
        block = block.astype(bf16).reshape(devices, cap, block.shape[1])
        out = lax.all_to_all(block, AXES, split_axis=0, concat_axis=0, tiled=True)
        return out.reshape(pool, block.shape[2])

    marked = jnp.concatenate([features, jnp.ones((rows, 128), bf16)], axis=1)
    got_feat = exchange(dotf(place, marked, 0, 0))
    leaf = jnp.sum(got_feat[:, :width], axis=0, dtype=f32) / math.sqrt(rows)
    coarse = lax.reduce_precision(leaf, 8, 7)
    halves = jnp.concatenate([coarse, leaf - coarse]).astype(bf16).reshape(1, cap, -1)
    halves = jnp.broadcast_to(halves, (devices,) + halves.shape[1:]).reshape(pool, -1)
    got_cot = exchange(
        jnp.concatenate([dotf(place, cotangent, 0, 0).astype(bf16), halves], axis=1)
    )

    firsts = packed((first_zero, first_one, first_two, first_three))
    seconds = packed((second_zero, second_one, second_two, second_three))
    degrees = degree_columns(chans)
    cols = 4 * nbr_count
    match = (np.arange(cols)[:, None] % 4 == degrees[None, :]).astype(np.float32)
    spread = jnp.asarray(np.concatenate([match, match], 0), bf16)
    collect = jnp.asarray(match.T, bf16)

    shape = jax.ShapeDtypeStruct
    params = pltpu.CompilerParams(vmem_limit_bytes=VMEM_LIMIT)
    edge_flops = 2 * pool * nbr_count * width * 1024
    base, feat, perm, nbr, rad, count = pl.pallas_call(
        functools.partial(forward_kernel, nbr_count, chans),
        out_shape=(
            shape((pool, width), f32),
            shape((pool, width), bf16),
            shape((pool, pool), bf16),
            shape((pool, nbr_count), f32),
            shape((pool, 2 * cols), bf16),
            shape((1, 1), jnp.int32),
        ),
        in_specs=vmem(6),
        out_specs=tuple(vmem(5)) + (pl.BlockSpec(memory_space=pltpu.SMEM),),
        compiler_params=params,
        cost_estimate=pl.CostEstimate(
            flops=edge_flops, bytes_accessed=8 << 20, transcendentals=pool * nbr_count * width
        ),
        name="edge_forward",
    )(got_feat, neighbours, radial, spread, firsts, seconds)

    tiles = got_cot[:, width:].reshape(devices, 2, cap // 2, -1)
    tiles = jnp.sum(tiles, axis=1, dtype=f32)
    tiles = tiles.reshape(size_x, size_y, size_z, 16, chans)
    index_x, index_y, index_z = (lax.axis_index(a) for a in AXES)
    root_w = couple_root[index_x] * (jnp.arange(size_x) != index_x)[:, None, None]
    branch_w = couple_branch[index_y] * (jnp.arange(size_y) != index_y)[:, None, None]
    leaf_w = couple_leaf[index_z] * (jnp.arange(size_z) != index_z)[:, None, None]
    branches = jnp.einsum("zpq,xyzqc->xypc", lift_leaf, tiles, precision=hp)
    roots = jnp.einsum("ypq,xyqc->xpc", lift_branch, branches, precision=hp)
    local1 = jnp.einsum("xpq,xqc->pc", root_w, roots, precision=hp)
    local2 = jnp.einsum("qp,qc->pc", lift_branch[index_y], local1, precision=hp) + jnp.einsum(
        "ypq,yqc->pc", branch_w, branches[index_x], precision=hp
    )
    local3 = jnp.einsum("qp,qc->pc", lift_leaf[index_z], local2, precision=hp) + jnp.einsum(
        "zpq,zqc->pc", leaf_w, tiles[index_x, index_y], precision=hp
    )
    out_c = (base + feat.astype(f32) * local3.reshape(1, width)).astype(bf16)
    returned = exchange(dotf(perm, out_c, 0, 0))

    grads = pl.pallas_call(
        functools.partial(backward_kernel, nbr_count, chans),
        out_shape=shape((cols, pool), f32),
        in_specs=[pl.BlockSpec(memory_space=pltpu.SMEM)] + vmem(9),
        out_specs=vmem(1)[0],
        scratch_shapes=[pltpu.VMEM((pool, width), f32), pltpu.VMEM((pool, cols), f32)],
        compiler_params=params,
        cost_estimate=pl.CostEstimate(
            flops=2 * edge_flops, bytes_accessed=8 << 20, transcendentals=pool * nbr_count * width
        ),
        name="edge_backward",
    )(count, got_cot, feat, perm, nbr, rad, spread, collect, firsts, seconds)

    updated = dotf(place, returned).astype(bf16)
    return (updated, grads)


def solution(mesh):
    split = P(AXES, None)
    across = P(None, AXES)
    placed = (split, split, split, across, across) + (P(),) * 13
    return jax.shard_map(
        shards,
        mesh=mesh,
        in_specs=placed,
        out_specs=(split, across),
        check_vma=False,
    )
```
